512 devices in a mesh: video: 8 (over z_lo), cache: 16 (over x, z_hi, core), head: 4 (over y).
Axes of the slice: x: 4, y: 4, z: 16 (z_hi: 2, z_lo: 8; z = z_hi * 8 + z_lo), core: 2. Of those that a mesh axis runs over, the one named last changes fastest.
Arguments:
- queries: bfloat16 [8192, 6144], P(('video', 'cache'), 'head'), parts along dimension 0, may hold values from -6 to 6
- group_keys: bfloat16 [8192, 6144], P(('video', 'cache'), 'head'), parts along dimension 0, may hold values from -6 to 6
- group_values: bfloat16 [8192, 6144], P(('video', 'cache'), 'head'), parts along dimension 0, may hold values from -6 to 6
- cache_keys: bfloat16 [65536, 6144], P(('video', 'cache'), 'head'), parts along dimension 0, may hold values from -6 to 6
- cache_values: bfloat16 [65536, 6144], P(('video', 'cache'), 'head'), parts along dimension 0, may hold values from -6 to 6
- block_mask: int32 [128, 64], P('video', 'cache'), parts along dimension 0, may hold values from 0 to 1, as said below
- gain: bfloat16 [6144], replicated, may hold values from 0.5 to 1.5
Outputs:
- normed: bfloat16 [8192, 6144], P(('video', 'cache', 'head')), parts along dimension 0
The draws below stay inside these ranges and needn't reach their ends.
There are 8 independent parts, one for each index of `video`. The reference program is written for one: setup_inputs(seed, part) draws one part's arguments, and reference() takes and returns one part's arrays. A program takes and returns all parts, laid end to end along the dimension named above; an argument that names none is the same for every part. Nothing has to cross between parts.
Inputs may be any that keep to these rules, and one draw needn't show every extreme that they name: `block_mask`: each cache shard's 4 blocks have their own density of ones, from one in eight to seven in eight.
All inputs are finite; a program needn't handle non-finite values.
Results may differ from the reference program's by a relative error of at most 0.025.
Values may be sent and summed in bfloat16 or wider, within the bound.
No kernel may reach another device: no remote copies, remote signals or barrier semaphores. Data moves between devices by JAX's collectives and lax.ppermute only.
A program may use at most 128 MiB of HBM per device.

```python
import jax
import jax.numpy as jnp
from jax import lax

D = 6144
HEADS = 48
HEAD_DIM = 128
Q_DEV = 64
KB_DEV = 4
BLOCK = 128
TILES = 16
BLOCKS = 64
Q_TOK = 1024
CACHE_TOK = 8192


def draw_queries(key, part):
    key = jax.random.fold_in(key, 5)
    sample = jnp.clip(jax.random.normal(key, (Q_TOK, D)), -6.0, 6.0)
    return sample.astype(jnp.bfloat16)


def draw_group_keys(key, part):
    key = jax.random.fold_in(key, 7)
    sample = jnp.clip(jax.random.normal(key, (Q_TOK, D)), -6.0, 6.0)
    return sample.astype(jnp.bfloat16)


def draw_cache_keys(key, part):
    key = jax.random.fold_in(key, 13)
    sample = jnp.clip(jax.random.normal(key, (CACHE_TOK, D)), -6.0, 6.0)
    return sample.astype(jnp.bfloat16)


def draw_block_mask(key, part):
    key = jax.random.fold_in(key, 9)
    key_density, key_cells = jax.random.split(key)
    density = jax.random.randint(key_density, (TILES,), 1, 8)
    cells = jax.random.randint(key_cells, (TILES, BLOCKS), 0, 8)
    shard_of = jnp.arange(BLOCKS) // KB_DEV
    return (cells < density[shard_of][None, :]).astype(jnp.int32)


def block_levels(key, shape, pieces, low, top_value):
    def one(dim, parts):
        steps = jax.random.uniform(jax.random.fold_in(jax.random.fold_in(key, 6), dim), (parts,), jnp.float32, low / len(pieces), top_value / len(pieces))
        return jnp.repeat(jnp.exp(steps), shape[dim] // parts).reshape((-1,) + (1,) * (len(shape) - dim - 1))

    loudness = one(*pieces[0])
    for cut in pieces[1:]:
        loudness = loudness * one(*cut)
    return loudness


def normal_values(key, dims, scale, bound, cuts=(), kind=jnp.bfloat16):
    entries = jax.random.normal(key, dims, jnp.float32) * scale
    if len(cuts) > 0:
        entries = block_levels(key, dims, cuts, -0.22, 0.18) * entries
    return jnp.clip(entries, min=-bound, max=bound).astype(kind)


def setup_inputs(seed: int = 0, part: int = 0) -> dict:
    keys = jax.random.split(jax.random.key(seed), 8)
    part_keys = jax.random.split(jax.random.fold_in(keys[7], part), 8)
    return {
        "queries": draw_queries(jax.random.fold_in(jax.random.fold_in(keys[7], part), 71), part),
        "group_keys": draw_group_keys(jax.random.fold_in(jax.random.fold_in(keys[7], part), 71), part),
        "group_values": normal_values(part_keys[2], (Q_TOK, D), 1.0, 6.0, ((0, 16), (1, 4))),
        "cache_keys": draw_cache_keys(jax.random.fold_in(jax.random.fold_in(keys[7], part), 71), part),
        "cache_values": normal_values(part_keys[4], (CACHE_TOK, D), 1.0, 6.0, ((0, 16), (1, 4))),
        "block_mask": draw_block_mask(jax.random.fold_in(jax.random.fold_in(keys[7], part), 71), part),
        "gain": jnp.clip(1.0 + 0.1 * jax.random.normal(keys[6], (D,), jnp.float32), 0.5, 1.5).astype(jnp.bfloat16),
    }


NEG = -1e+30

def reference(queries, group_keys, group_values, cache_keys, cache_values, block_mask, gain):
    scale = HEAD_DIM ** (-0.5)
    keys_cached = cache_keys.astype(jnp.float32).reshape(CACHE_TOK, HEADS, HEAD_DIM)
    values_cached = cache_values.astype(jnp.float32).reshape(CACHE_TOK, HEADS, HEAD_DIM)

    def one_tile(tile_index):
        start = (tile_index * Q_DEV).astype(jnp.int32)
        query_rows = lax.dynamic_slice_in_dim(queries, start, Q_DEV, 0).astype(jnp.float32).reshape(Q_DEV, HEADS, HEAD_DIM)
        own_keys = lax.dynamic_slice_in_dim(group_keys, start, Q_DEV, 0).astype(jnp.float32).reshape(Q_DEV, HEADS, HEAD_DIM)
        own_values = lax.dynamic_slice_in_dim(group_values, start, Q_DEV, 0).astype(jnp.float32).reshape(Q_DEV, HEADS, HEAD_DIM)
        all_keys = jnp.concatenate([own_keys, keys_cached], axis=0)
        all_values = jnp.concatenate([own_values, values_cached], axis=0)
        mask_row = block_mask[tile_index]
        visible = jnp.concatenate([jnp.ones((Q_DEV,), jnp.int32), jnp.repeat(mask_row, BLOCK)]) > 0
        scores = jnp.einsum('qhd,khd->hqk', query_rows, all_keys) * scale
        scores = jnp.where(visible[None, None, :], scores, NEG)
        row_max = lax.optimization_barrier(jnp.max(scores, axis=-1, keepdims=True))
        weights = jnp.where(visible[None, None, :], jnp.exp(scores - row_max), 0.0)
        denominator = lax.optimization_barrier(jnp.sum(weights, axis=-1))
        rounded = weights.astype(jnp.bfloat16).astype(jnp.float32)
        numerator = jnp.einsum('hqk,khd->qhd', rounded, all_values)
        attended = numerator / jnp.transpose(denominator)[:, :, None]
        return attended.astype(jnp.bfloat16).reshape(Q_DEV, D)
    attended = lax.map(one_tile, jnp.arange(TILES, dtype=jnp.int32)).reshape(Q_TOK, D)
    rows = attended.astype(jnp.float32)
    square_mean = lax.optimization_barrier(jnp.mean(rows * rows, axis=-1, keepdims=True))
    normed = rows * lax.rsqrt(square_mean + 1e-06) * gain.astype(jnp.float32)
    return normed.astype(jnp.bfloat16)
```

```python
import jax
import jax.numpy as jnp
from jax import lax
from jax.experimental import pallas as pl
from jax.experimental.pallas import tpu as pltpu
from jax.sharding import Mesh
from jax.sharding import PartitionSpec as P

HEAD_DIM = 128
BLOCK = 128
HEADS_X = 3
Q_ROWS = 64
ROWS = 8 * Q_ROWS
TOK = 512
LOG2_SCALE = HEAD_DIM ** (-0.5) * 1.4426950408889634
NEG = -1e30
KEYS = slice(0, TOK)
VALUES = slice(TOK, 2 * TOK)
HIDDEN = slice(2 * TOK, 2 * TOK + 16)
OWN_KEYS = slice(2 * TOK + 16, 2 * TOK + 16 + Q_ROWS)
OWN_VALUES = slice(2 * TOK + 16 + Q_ROWS, 2 * TOK + 16 + 2 * Q_ROWS)
QUERIES = slice(2 * TOK + 16 + 2 * Q_ROWS, 2 * TOK + 16 + 3 * Q_ROWS)
PACKET = 2 * TOK + 16 + 3 * Q_ROWS
STATS = 8
NT = (((1,), (1,)), ((), ()))
NN = (((1,), (0,)), ((), ()))
VMEM = pl.BlockSpec(memory_space=pltpu.VMEM)
SMEM = pl.BlockSpec(memory_space=pltpu.SMEM)
PARAMS = pltpu.CompilerParams(vmem_limit_bytes=60 * 2**20)


def with_ones(values):
    return jnp.concatenate([values, jnp.ones((values.shape[0], HEAD_DIM), jnp.bfloat16)], 1)


def matmul(a, b, dims):
    return lax.dot_general(a, b, dims, preferred_element_type=jnp.float32)


def fold(scores, values, top, total):
    new_top = jnp.maximum(top, jnp.max(scores, axis=1, keepdims=True))
    weights = jnp.exp2((scores - new_top) * LOG2_SCALE).astype(jnp.bfloat16)
    factor = jnp.exp2((top - new_top) * LOG2_SCALE)
    return new_top, total * factor + matmul(weights, with_ones(values), NN)


def pack_kernel(k_ref, v_ref, mask_ref, own_k_ref, own_v_ref, q_ref, out_ref):
    hidden = jnp.where(mask_ref[...] > 0, 0.0, NEG)
    hidden = jnp.concatenate([hidden, jnp.zeros((16, HEAD_DIM - 4), jnp.float32)], 1)
    out_ref[0, KEYS, :] = k_ref[...]
    out_ref[0, VALUES, :] = v_ref[...]
    out_ref[0, HIDDEN, :] = jnp.concatenate([hidden.astype(jnp.bfloat16)] * HEADS_X, 1)
    out_ref[0, OWN_KEYS, :] = own_k_ref[...]
    out_ref[0, OWN_VALUES, :] = own_v_ref[...]
    out_ref[0, QUERIES, :] = q_ref[...]


def pack(keys, values, mask, own_keys, own_values, queries):
    width = HEADS_X * HEAD_DIM
    big = pl.BlockSpec((TOK, width), lambda x: (0, x))
    small = pl.BlockSpec((Q_ROWS, width), lambda x: (0, x))
    return pl.pallas_call(
        pack_kernel,
        grid=(4,),
        in_specs=[big, big, pl.BlockSpec((16, 4), lambda x: (0, 0)), small, small, small],
        out_specs=pl.BlockSpec((1, PACKET, width), lambda x: (x, 0, 0)),
        out_shape=jax.ShapeDtypeStruct((4, PACKET, width), jnp.bfloat16),
        compiler_params=PARAMS,
    )(keys, values, mask, own_keys, own_values, queries)


def attend_kernel(place_ref, *refs):
    far, (mine_ref, theirs_ref, out_ref, log_ref, logs_ref, hidden_ref, bias_ref) = refs[:4], refs[4:]
    head = pl.program_id(0)
    core, z = place_ref[4], place_ref[5]
    caches = (mine_ref, theirs_ref)
    where = [(t, z) if t < 4 else (place_ref[t - 4], 1 - z) for t in range(8)]

    @pl.when(head == 0)
    def _():
        for src in range(8):
            hidden_ref[src] = caches[src % 2][src // 2, HIDDEN, :].astype(jnp.float32)
            for t in range(8):
                x, z_tile = where[t]
                row = hidden_ref[src, pl.ds(x * 4 + z_tile * 2 + core, 1), :]
                for b in range(4):
                    bias_ref[src, t, b] = jnp.broadcast_to(row[:, b : b + 1], (8, HEAD_DIM))

    queries = jnp.concatenate(
        [mine_ref[x, QUERIES, :] for x in range(4)] + [tile[...] for tile in far], 0
    )
    top = jnp.full((ROWS, 1), -3e30, jnp.float32)
    total = jnp.zeros((ROWS, 2 * HEAD_DIM), jnp.float32)
    for src in range(8):
        cache = caches[src % 2]
        scores = matmul(queries, cache[src // 2, KEYS, :], NT)
        scores = jnp.concatenate(
            [
                jnp.concatenate(
                    [
                        (
                            scores[t * Q_ROWS : (t + 1) * Q_ROWS, b * BLOCK : (b + 1) * BLOCK].reshape(
                                8, 8, BLOCK
                            )
                            + bias_ref[src, t, b][None]
                        ).reshape(Q_ROWS, BLOCK)
                        for b in range(4)
                    ],
                    1,
                )
                for t in range(8)
            ],
            0,
        )
        top, total = fold(scores, cache[src // 2, VALUES, :], top, total)

    for t in range(8):
        rows = slice(t * Q_ROWS, (t + 1) * Q_ROWS)
        tile_top, tile_total = top[rows], total[rows]
        x, z_tile = where[t]
        if t < 4:
            scores = matmul(mine_ref[t, QUERIES, :], mine_ref[t, OWN_KEYS, :], NT)
            tile_top, tile_total = fold(scores, mine_ref[t, OWN_VALUES, :], tile_top, tile_total)
        den = tile_total[:, HEAD_DIM:]
        part = (tile_total[:, :HEAD_DIM] / den).astype(jnp.bfloat16)
        out_ref[pl.ds(z_tile * 16 + x * 4, 4)] = part.reshape(4, 16, HEAD_DIM)
        logs_ref[head, z_tile * 4 + x] = tile_top * LOG2_SCALE + jnp.log2(den)

    @pl.when(head == HEADS_X - 1)
    def _():
        lane = lax.broadcasted_iota(jnp.int32, (ROWS, HEAD_DIM), 1)
        logs = logs_ref[0].reshape(ROWS, HEAD_DIM)
        for j in range(1, HEADS_X):
            logs = jnp.where(lane == j, logs_ref[j].reshape(ROWS, HEAD_DIM), logs)
        log_ref[...] = jnp.transpose(logs)[:8]


def attend(place, far, mine, theirs):
    heads = HEADS_X
    tile = pl.BlockSpec((Q_ROWS, HEAD_DIM), lambda j: (0, j))
    cache = pl.BlockSpec((4, mine.shape[1], HEAD_DIM), lambda j: (0, 0, j))
    return pl.pallas_call(
        attend_kernel,
        grid=(heads,),
        in_specs=[SMEM] + [tile] * 4 + [cache] * 2,
        out_specs=[
            pl.BlockSpec((32, 16, HEAD_DIM), lambda j: (0, j, 0)),
            pl.BlockSpec((8, ROWS), lambda j: (0, 0)),
        ],
        out_shape=[
            jax.ShapeDtypeStruct((32, heads * 16, HEAD_DIM), jnp.bfloat16),
            jax.ShapeDtypeStruct((8, ROWS), jnp.float32),
        ],
        scratch_shapes=[
            pltpu.VMEM((heads, 8, Q_ROWS, HEAD_DIM), jnp.float32),
            pltpu.VMEM((8, 16, HEAD_DIM), jnp.float32),
            pltpu.VMEM((8, 8, 4, 8, HEAD_DIM), jnp.float32),
        ],
        compiler_params=PARAMS,
        cost_estimate=pl.CostEstimate(
            flops=heads * 4 * ROWS * 4096 * 128, bytes_accessed=heads * 2**21, transcendentals=heads * 2**21
        ),
    )(place, *far, mine, theirs)


def final_kernel(part_ref, log_ref, gain_ref, out_ref, joined):
    split = jnp.sum(log_ref[...].astype(jnp.float32), axis=1)
    logs = [split[:16], split[16:]]
    top = jnp.maximum(*logs)
    shares = [jnp.exp2(a - top) for a in logs]
    whole = 1.0 / (shares[0] + shares[1])
    shares = [jnp.transpose(a * whole) for a in shares]
    squares = jnp.zeros((16, HEAD_DIM), jnp.float32)
    for x in range(4):
        for y in range(4):
            src = x * 4 + y
            value = (
                shares[0][:48, src : src + 1] * part_ref[src].astype(jnp.float32)
                + shares[1][:48, src : src + 1] * part_ref[16 + src].astype(jnp.float32)
            )
            value = value.astype(jnp.bfloat16).astype(jnp.float32)
            for head in range(HEADS_X):
                place = (y * 12 + x * HEADS_X + head) * HEAD_DIM
                piece = value[head * 16 : (head + 1) * 16]
                joined[:, place : place + HEAD_DIM] = piece
                squares = squares + piece * piece
    mean = jnp.sum(squares, axis=1, keepdims=True) * (1.0 / 6144)
    out_ref[...] = (
        joined[...] * lax.rsqrt(mean + 1e-06) * gain_ref[...].astype(jnp.float32)
    ).astype(jnp.bfloat16)


def thirds(logs):
    high = lax.reduce_precision(logs, 8, 7)
    middle = lax.reduce_precision(logs - high, 8, 7)
    low = lax.reduce_precision(logs - high - middle, 8, 7)
    rows = jnp.stack([high, middle, low], 1).astype(jnp.bfloat16)
    return jnp.pad(rows, ((0, 0), (0, STATS - 3), (0, HEAD_DIM - logs.shape[1])))


def local(queries, group_keys, group_values, cache_keys, cache_values, block_mask, gain):
    me = lax.axis_index("x")
    core = lax.axis_index("core")
    width = HEADS_X * HEAD_DIM

    mine = pack(cache_keys, cache_values, block_mask, group_keys, group_values, queries)
    mine = lax.all_to_all(mine, "x", 0, 0, tiled=True)

    def send(turn):
        block = lax.dynamic_slice_in_dim(queries, ((me + turn) % 4) * width, width, 1)
        route = [(x * 2 + z, (x + turn) % 4 * 2 + 1 - z) for x in range(4) for z in range(2)]
        return lax.ppermute(block, ("x", "z"), route)

    far = [send(turn) for turn in range(4)]
    mine, far = lax.optimization_barrier((mine, far))
    theirs = lax.ppermute(mine, "core", [(0, 1), (1, 0)])
    place = jnp.stack([(me - turn) % 4 for turn in range(4)] + [core, lax.axis_index("z")])
    part, logs = attend(place.astype(jnp.int32), far, mine, theirs)
    logs = logs[:HEADS_X]
    logs = logs.reshape(HEADS_X, 32, 16).transpose(1, 0, 2).reshape(32, 48)
    block = jnp.concatenate([part, thirds(logs)], 1)
    block = lax.all_to_all(block, ("z", "x", "head"), 0, 0, tiled=True)

    return pl.pallas_call(
        final_kernel,
        in_specs=[VMEM] * 3,
        out_specs=VMEM,
        out_shape=jax.ShapeDtypeStruct((16, 48 * HEAD_DIM), jnp.bfloat16),
        scratch_shapes=[pltpu.VMEM((16, 48 * HEAD_DIM), jnp.float32)],
        compiler_params=PARAMS,
    )(block[:, :48], block[:, 48:], gain.reshape(1, 48 * HEAD_DIM))


def solution(mesh):
    fine = Mesh(mesh.devices.reshape(8, 4, 2, 2, 4), ("video", "x", "z", "core", "head"))
    rows = ("video", "x", "z", "core")
    return jax.shard_map(
        local,
        mesh=fine,
        in_specs=(P(rows, "head"),) * 5 + (P("video", ("x", "z", "core")), P()),
        out_specs=P((*rows, "head"), None),
        check_vma=False,
    )
```

```python
import jax
import jax.numpy as jnp
from jax import lax
from jax.experimental import pallas as pl
from jax.experimental.pallas import tpu as pltpu
from jax.sharding import Mesh
from jax.sharding import PartitionSpec as P

HEAD_DIM = 128
BLOCK = 128
HEADS_X = 3
Q_ROWS = 64
ROWS = 8 * Q_ROWS
TOK = 512
LOG2_SCALE = HEAD_DIM ** (-0.5) * 1.4426950408889634
NEG = -1e30
KEYS = slice(0, TOK)
VALUES = slice(TOK, 2 * TOK)
QUERIES = slice(2 * TOK, 2 * TOK + Q_ROWS)
HIDDEN = slice(2 * TOK + Q_ROWS, 2 * TOK + Q_ROWS + 16)
PACKET = 2 * TOK + Q_ROWS + 16
LOGS = slice(HEADS_X * Q_ROWS, HEADS_X * Q_ROWS + 16)
FAR = HEADS_X * Q_ROWS + 16
NT = (((1,), (1,)), ((), ()))
NN = (((1,), (0,)), ((), ()))
VMEM = pl.BlockSpec(memory_space=pltpu.VMEM)
SMEM = pl.BlockSpec(memory_space=pltpu.SMEM)
PARAMS = pltpu.CompilerParams(vmem_limit_bytes=40 * 2**20)


def with_ones(values):
    return jnp.concatenate([values, jnp.ones((values.shape[0], HEAD_DIM), jnp.bfloat16)], 1)


def matmul(a, b, dims):
    return lax.dot_general(a, b, dims, preferred_element_type=jnp.float32)


def fold(scores, values, top, total):
    new_top = jnp.maximum(top, jnp.max(scores, axis=1, keepdims=True))
    weights = jnp.exp2((scores - new_top) * LOG2_SCALE).astype(jnp.bfloat16)
    factor = jnp.exp2((top - new_top) * LOG2_SCALE)
    return new_top, total * factor + matmul(weights, with_ones(values), NN)


def pack_kernel(place_ref, k_ref, v_ref, mask_ref, q_ref, own_k_ref, own_v_ref, out_ref, *turn_refs):
    hidden = jnp.where(mask_ref[...] > 0, 0.0, NEG)
    hidden = jnp.concatenate([hidden, hidden], 0)
    hidden = jnp.concatenate([hidden, jnp.zeros((8, HEAD_DIM - 16), jnp.float32)], 1)
    hidden = jnp.transpose(hidden)[:16]
    hidden = jnp.concatenate([hidden, jnp.zeros((16, HEAD_DIM - 8), jnp.float32)], 1)
    out_ref[0, KEYS, :] = k_ref[...]
    out_ref[0, VALUES, :] = v_ref[...]
    out_ref[0, HIDDEN, :] = jnp.concatenate([hidden.astype(jnp.bfloat16)] * HEADS_X, 1)
    out_ref[0, QUERIES, :] = q_ref[...]
    for turn in range(4):

        @pl.when(pl.program_id(0) == place_ref[6 + turn])
        def _(turn=turn):
            rows = slice(turn % 2 * Q_ROWS, (turn % 2 + 1) * Q_ROWS)
            turn_refs[turn // 2][rows, :] = q_ref[...]
            turn_refs[2 + turn][:Q_ROWS, :] = own_k_ref[...]
            turn_refs[2 + turn][Q_ROWS:, :] = own_v_ref[...]


def pack(place, keys, values, mask, queries, own_keys, own_values):
    width = HEADS_X * HEAD_DIM
    big = pl.BlockSpec((TOK, width), lambda x: (0, x))
    small = pl.BlockSpec((Q_ROWS, width), lambda x: (0, x))
    sizes = [(2 * Q_ROWS, width)] * 6
    packet, *turns = pl.pallas_call(
        pack_kernel,
        grid=(4,),
        in_specs=[SMEM, big, big, pl.BlockSpec((4, 16), lambda x: (0, 0)), small, small, small],
        out_specs=[pl.BlockSpec((1, PACKET, width), lambda x: (x, 0, 0))]
        + [pl.BlockSpec(size, lambda x: (0, 0)) for size in sizes],
        out_shape=[jax.ShapeDtypeStruct((4, PACKET, width), jnp.bfloat16)]
        + [jax.ShapeDtypeStruct(size, jnp.bfloat16) for size in sizes],
        compiler_params=pltpu.CompilerParams(vmem_limit_bytes=62 * 2**20),
    )(place, keys, values, mask.T, queries, own_keys, own_values)
    return packet, turns[:2], turns[2:]


def put_hidden(cache_ref, hidden_ref):
    for src in range(4):
        hidden = cache_ref[src, HIDDEN, :].astype(jnp.float32)
        for b in range(4):
            hidden_ref[src, b] = jnp.broadcast_to(hidden[:, b : b + 1], (16, HEAD_DIM))


def over_cache(queries, rows, cache_ref, hidden_ref, top, total):
    product = matmul(queries, cache_ref[0, KEYS, :], NT)
    for src in range(4):
        scores = jnp.concatenate(
            [
                jnp.concatenate(
                    [
                        product[t * Q_ROWS : (t + 1) * Q_ROWS, b * BLOCK : (b + 1) * BLOCK]
                        + jnp.broadcast_to(hidden_ref[src, b, pl.ds(row, 1), :], (Q_ROWS, BLOCK))
                        for b in range(4)
                    ],
                    1,
                )
                for t, row in enumerate(rows)
            ],
            0,
        )
        if src < 3:
            product = matmul(queries, cache_ref[src + 1, KEYS, :], NT)
        top, total = fold(scores, cache_ref[src, VALUES, :], top, total)
    return top, total


def far_rows(place_ref):
    return [place_ref[t] * 4 + (1 - place_ref[5]) * 2 + place_ref[4] for t in range(4)]


def first_kernel(place_ref, f0, f1, f2, f3, mine_ref, top_ref, total_ref, hidden_ref):
    @pl.when(pl.program_id(0) == 0)
    def _():
        put_hidden(mine_ref, hidden_ref)

    queries = jnp.concatenate([tile[...] for tile in (f0, f1, f2, f3)], 0)
    top = jnp.full((4 * Q_ROWS, 1), -3e30, jnp.float32)
    total = jnp.zeros((4 * Q_ROWS, 2 * HEAD_DIM), jnp.float32)
    top, total = over_cache(queries, far_rows(place_ref), mine_ref, hidden_ref, top, total)
    top_ref[0] = jnp.broadcast_to(top, (4 * Q_ROWS, HEAD_DIM))
    total_ref[0] = total


def far_kernel(
    place_ref, f0, f1, f2, f3, theirs_ref, top_ref, total_ref, out_ref, logs_ref, hidden_ref
):
    head = pl.program_id(0)

    @pl.when(head == 0)
    def _():
        put_hidden(theirs_ref, hidden_ref)

    queries = jnp.concatenate([tile[...] for tile in (f0, f1, f2, f3)], 0)
    top = jnp.max(top_ref[0], axis=1, keepdims=True)
    top, total = over_cache(queries, far_rows(place_ref), theirs_ref, hidden_ref, top, total_ref[0])
    den = total[:, HEAD_DIM:]
    part = total[:, :HEAD_DIM] / den
    logs = top * LOG2_SCALE + jnp.log2(den)
    part = part.astype(jnp.bfloat16)
    for t in range(4):
        rows = slice(t * Q_ROWS, (t + 1) * Q_ROWS)
        out_ref[place_ref[t], pl.ds(pl.multiple_of(head * Q_ROWS, Q_ROWS), Q_ROWS), :] = part[rows]
        logs_ref[head, place_ref[t]] = logs[rows]

    @pl.when(head == HEADS_X - 1)
    def _():
        lane = lax.broadcasted_iota(jnp.int32, (Q_ROWS, HEAD_DIM), 1)
        for x in range(4):
            logs = jnp.zeros((Q_ROWS, HEAD_DIM), jnp.float32)
            for j in range(HEADS_X):
                logs = jnp.where(lane == j, logs_ref[j, x], logs)
            logs = jnp.transpose(logs)[:8]
            high = logs.astype(jnp.bfloat16).astype(jnp.float32)
            middle = (logs - high).astype(jnp.bfloat16).astype(jnp.float32)
            low = logs - high - middle
            rows = jnp.concatenate([high[:4], middle[:4], low], 0)
            rows = jnp.concatenate([rows, jnp.zeros((16, HEAD_DIM - Q_ROWS), jnp.float32)], 1)
            out_ref[x, LOGS, :] = rows.astype(jnp.bfloat16)


def near_kernel(place_ref, mine_ref, theirs_ref, top_ref, total_ref, hidden_ref):
    @pl.when(pl.program_id(0) == 0)
    def _():
        put_hidden(mine_ref, hidden_ref.at[0])
        put_hidden(theirs_ref, hidden_ref.at[1])

    mask_rows = [t * 4 + place_ref[5] * 2 + place_ref[4] for t in range(4)]
    queries = jnp.concatenate([mine_ref[x, QUERIES, :] for x in range(4)], 0)
    top = jnp.full((4 * Q_ROWS, 1), -3e30, jnp.float32)
    total = jnp.zeros((4 * Q_ROWS, 2 * HEAD_DIM), jnp.float32)
    top, total = over_cache(queries, mask_rows, mine_ref, hidden_ref.at[0], top, total)
    top, total = over_cache(queries, mask_rows, theirs_ref, hidden_ref.at[1], top, total)
    top_ref[0] = jnp.broadcast_to(top, (4 * Q_ROWS, HEAD_DIM)).reshape(4, Q_ROWS, HEAD_DIM)
    total_ref[0] = total.reshape(4, Q_ROWS, 2 * HEAD_DIM)


def own_kernel(place_ref, q_ref, o0, o1, o2, o3, top_ref, total_ref, out_ref, log_ref):
    for t, own_ref in enumerate((o0, o1, o2, o3)):
        x = place_ref[t]
        for j in range(HEADS_X):
            cols = slice(j * HEAD_DIM, (j + 1) * HEAD_DIM)
            scores = matmul(q_ref[x, :, cols], own_ref[:Q_ROWS, cols], NT)
            top = jnp.max(top_ref[j, x], axis=1, keepdims=True)
            top, total = fold(scores, own_ref[Q_ROWS:, cols], top, total_ref[j, x])
            den = total[:, HEAD_DIM:]
            out_ref[j, x] = total[:, :HEAD_DIM] / den
            log_ref[j, x] = top * LOG2_SCALE + jnp.log2(den)


def join_kernel(near_ref, near_log_ref, far_ref, out_ref):
    for x in range(4):
        logs = far_ref[x, LOGS, :].astype(jnp.float32)
        logs = logs[:4] + logs[4:8] + logs[8:12]
        logs = jnp.transpose(jnp.concatenate([logs, logs], 0))
        for j in range(HEADS_X):
            far_log = logs[:Q_ROWS, j : j + 1]
            near_log = near_log_ref[j, x]
            top = jnp.maximum(near_log, far_log)
            near_share, far_share = jnp.exp2(near_log - top), jnp.exp2(far_log - top)
            far = far_ref[x, j * Q_ROWS : (j + 1) * Q_ROWS, :].astype(jnp.float32)
            value = (near_ref[j, x] * near_share + far * far_share) / (near_share + far_share)
            value = value.astype(jnp.bfloat16)
            for y in range(4):
                out_ref[x * 4 + y, j * 16 : (j + 1) * 16, :] = value[y * 16 : (y + 1) * 16]


def norm_kernel(part_ref, gain_ref, out_ref):
    squares = jnp.zeros((16, HEAD_DIM), jnp.float32)
    for src in range(16):
        value = part_ref[src].astype(jnp.float32)
        value = value * value
        for j in range(HEADS_X):
            squares = squares + value[j * 16 : (j + 1) * 16]
    mean = jnp.sum(squares, axis=1, keepdims=True) * (1.0 / 6144)
    factor = lax.rsqrt(mean + 1e-06)
    for x in range(4):
        for y in range(4):
            for j in range(HEADS_X):
                value = part_ref[x * 4 + y, j * 16 : (j + 1) * 16, :].astype(jnp.float32)
                place = (y * 12 + x * HEADS_X + j) * HEAD_DIM
                cols = slice(place, place + HEAD_DIM)
                gain = gain_ref[:, cols].astype(jnp.float32)
                out_ref[:, cols] = (value * factor * gain).astype(jnp.bfloat16)


def attend(place, far, own, mine, theirs):
    heads = HEADS_X
    tiles = [pl.BlockSpec((Q_ROWS, HEAD_DIM), lambda j, row=row: (row, j)) for row in (0, 0, 0, 1)]
    cache = pl.BlockSpec((4, PACKET, HEAD_DIM), lambda j: (0, 0, j))

    state = [
        pl.BlockSpec((1, 4 * Q_ROWS, width), lambda j: (j, 0, 0)) for width in (HEAD_DIM, 2 * HEAD_DIM)
    ]
    state_shape = [
        jax.ShapeDtypeStruct((heads, 4 * Q_ROWS, width), jnp.float32) for width in (HEAD_DIM, 2 * HEAD_DIM)
    ]
    hidden = pltpu.VMEM((4, 4, 16, HEAD_DIM), jnp.float32)

    def common(keys):
        return dict(
            grid=(heads,),
            compiler_params=PARAMS,
            cost_estimate=pl.CostEstimate(
                flops=heads * 16 * Q_ROWS * keys * 128,
                bytes_accessed=heads * keys * 2**9,
                transcendentals=heads * 4 * Q_ROWS * keys,
            ),
        )

    top, total = pl.pallas_call(
        first_kernel,
        in_specs=[SMEM] + tiles + [cache],
        out_specs=state,
        out_shape=state_shape,
        scratch_shapes=[hidden],
        **common(2048),
    )(place, *far, mine)
    far_out = pl.pallas_call(
        far_kernel,
        in_specs=[SMEM] + tiles + [cache] + state,
        out_specs=pl.BlockSpec((4, FAR, HEAD_DIM), lambda j: (0, 0, 0)),
        out_shape=jax.ShapeDtypeStruct((4, FAR, HEAD_DIM), jnp.bfloat16),
        scratch_shapes=[pltpu.VMEM((heads, 4, Q_ROWS, HEAD_DIM), jnp.float32), hidden],
        **common(2048),
    )(place, *far, theirs, top, total)
    far_out, own = lax.optimization_barrier((far_out, own))
    far_out = lax.ppermute(far_out, "z", [(0, 1), (1, 0)])
    own = [own[0]] + [
        lax.ppermute(own[turn], "x", [(x, (x + turn) % 4) for x in range(4)]) for turn in range(1, 4)
    ]
    near = [
        pl.BlockSpec((1, 4, Q_ROWS, width), lambda j: (j, 0, 0, 0)) for width in (HEAD_DIM, 2 * HEAD_DIM)
    ]
    top, total = pl.pallas_call(
        near_kernel,
        in_specs=[SMEM, cache, cache],
        out_specs=near,
        out_shape=[
            jax.ShapeDtypeStruct((heads, 4, Q_ROWS, width), jnp.float32) for width in (HEAD_DIM, 2 * HEAD_DIM)
        ],
        scratch_shapes=[pltpu.VMEM((2, 4, 4, 16, HEAD_DIM), jnp.float32)],
        **common(4096),
    )(place, mine, theirs)

    def whole(shape):
        return pl.BlockSpec(shape, lambda i: (0,) * len(shape))

    near_shape = (heads, 4, Q_ROWS, HEAD_DIM)
    near_out, near_log = pl.pallas_call(
        own_kernel,
        grid=(1,),
        in_specs=[
            SMEM,
            pl.BlockSpec((4, Q_ROWS, heads * HEAD_DIM), lambda i: (0, QUERIES.start // Q_ROWS, 0)),
            *[whole((2 * Q_ROWS, heads * HEAD_DIM))] * 4,
            whole(top.shape),
            whole(total.shape),
        ],
        out_specs=[whole(near_shape)] * 2,
        out_shape=[jax.ShapeDtypeStruct(near_shape, jnp.float32)] * 2,
        compiler_params=PARAMS,
    )(place, mine, *own, top, total)
    return pl.pallas_call(
        join_kernel,
        in_specs=[VMEM] * 3,
        out_specs=VMEM,
        out_shape=jax.ShapeDtypeStruct((16, heads * 16, HEAD_DIM), jnp.bfloat16),
        compiler_params=PARAMS,
    )(near_out, near_log, far_out)


def local(queries, group_keys, group_values, cache_keys, cache_values, block_mask, gain):
    me, z, core = (lax.axis_index(axis) for axis in ("x", "z", "core"))
    place = [(me - turn) % 4 for turn in range(4)] + [core, z] + [(me + turn) % 4 for turn in range(4)]
    place = jnp.stack(place).astype(jnp.int32)

    packet, blocks, own = pack(
        place, cache_keys, cache_values, block_mask, queries, group_keys, group_values
    )
    mine = lax.all_to_all(packet, "x", 0, 0, tiled=True)

    def send(block, turn):
        route = [(x * 2 + z, (x + turn) % 4 * 2 + 1 - z) for x in range(4) for z in range(2)]
        return lax.ppermute(block, ("x", "z"), route)

    far = [send(blocks[0], 0), send(blocks[1], 2)]
    odd = jnp.concatenate([block[Q_ROWS:] for block in far], 0)
    odd = lax.ppermute(odd, "x", [(x, (x + 1) % 4) for x in range(4)])
    mine, far = lax.optimization_barrier((mine, [far[0], odd, far[1]]))
    far = [pltpu.with_memory_space_constraint(a, pltpu.HBM) for a in far]
    far.append(far[1])
    theirs = lax.ppermute(mine, "core", [(0, 1), (1, 0)])
    block = attend(place, far, own, mine, theirs)
    block = lax.all_to_all(block, ("x", "head"), 0, 0, tiled=True)
    return pl.pallas_call(
        norm_kernel,
        in_specs=[VMEM] * 2,
        out_specs=VMEM,
        out_shape=jax.ShapeDtypeStruct((16, 48 * HEAD_DIM), jnp.bfloat16),
        compiler_params=PARAMS,
    )(block, gain.reshape(1, 48 * HEAD_DIM))


def solution(mesh):
    fine = Mesh(mesh.devices.reshape(8, 4, 2, 2, 4), ("video", "x", "z", "core", "head"))
    rows = ("video", "x", "z", "core")
    return jax.shard_map(
        local,
        mesh=fine,
        in_specs=(P(rows, "head"),) * 5 + (P("video", ("x", "z", "core")), P()),
        out_specs=P((*rows, "head"), None),
        check_vma=False,
    )
```

```python
import jax
import jax.numpy as jnp
from jax import lax
from jax.experimental import pallas as pl
from jax.experimental.pallas import tpu as pltpu
from jax.sharding import Mesh
from jax.sharding import PartitionSpec as P

HEAD_DIM = 128
BLOCK = 128
HEADS_X = 3
Q_ROWS = 64
ROWS = 8 * Q_ROWS
TOK = 512
LOG2_SCALE = HEAD_DIM ** (-0.5) * 1.4426950408889634
NEG = -1e30
KEYS = slice(0, TOK)
VALUES = slice(TOK, 2 * TOK)
QUERIES = slice(2 * TOK, 2 * TOK + Q_ROWS)
HIDDEN = slice(2 * TOK + Q_ROWS, 2 * TOK + Q_ROWS + 16)
PACKET = 2 * TOK + Q_ROWS + 16
LOGS = slice(HEADS_X * Q_ROWS, HEADS_X * Q_ROWS + 16)
FAR = HEADS_X * Q_ROWS + 16
NT = (((1,), (1,)), ((), ()))
NN = (((1,), (0,)), ((), ()))
VMEM = pl.BlockSpec(memory_space=pltpu.VMEM)
SMEM = pl.BlockSpec(memory_space=pltpu.SMEM)
PARAMS = pltpu.CompilerParams(vmem_limit_bytes=40 * 2**20)


def with_ones(values):
    return jnp.concatenate([values, jnp.ones((values.shape[0], HEAD_DIM), jnp.bfloat16)], 1)


def matmul(a, b, dims):
    return lax.dot_general(a, b, dims, preferred_element_type=jnp.float32)


def fold(scores, values, top, total):
    new_top = jnp.maximum(top, jnp.max(scores, axis=1, keepdims=True))
    weights = jnp.exp2((scores - new_top) * LOG2_SCALE).astype(jnp.bfloat16)
    factor = jnp.exp2((top - new_top) * LOG2_SCALE)
    return new_top, total * factor + matmul(weights, with_ones(values), NN)


def pack_kernel(place_ref, k_ref, v_ref, mask_ref, q_ref, own_k_ref, own_v_ref, out_ref, *turn_refs):
    hidden = jnp.where(mask_ref[...] > 0, 0.0, NEG)
    hidden = jnp.concatenate([hidden, hidden], 0)
    hidden = jnp.concatenate([hidden, jnp.zeros((8, HEAD_DIM - 16), jnp.float32)], 1)
    hidden = jnp.transpose(hidden)[:16]
    hidden = jnp.concatenate([hidden, jnp.zeros((16, HEAD_DIM - 8), jnp.float32)], 1)
    out_ref[0, KEYS, :] = k_ref[...]
    out_ref[0, VALUES, :] = v_ref[...]
    out_ref[0, HIDDEN, :] = jnp.concatenate([hidden.astype(jnp.bfloat16)] * HEADS_X, 1)
    out_ref[0, QUERIES, :] = q_ref[...]
    for turn in range(4):

        @pl.when(pl.program_id(0) == place_ref[6 + turn])
        def _(turn=turn):
            rows = slice(turn % 2 * Q_ROWS, (turn % 2 + 1) * Q_ROWS)
            turn_refs[turn // 2][rows, :] = q_ref[...]
            turn_refs[2 + turn][:Q_ROWS, :] = own_k_ref[...]
            turn_refs[2 + turn][Q_ROWS:, :] = own_v_ref[...]


def pack(place, keys, values, mask, queries, own_keys, own_values):
    width = HEADS_X * HEAD_DIM
    big = pl.BlockSpec((TOK, width), lambda x: (0, x))
    small = pl.BlockSpec((Q_ROWS, width), lambda x: (0, x))
    sizes = [(2 * Q_ROWS, width)] * 6
    packet, *turns = pl.pallas_call(
        pack_kernel,
        grid=(4,),
        in_specs=[SMEM, big, big, pl.BlockSpec((4, 16), lambda x: (0, 0)), small, small, small],
        out_specs=[pl.BlockSpec((1, PACKET, width), lambda x: (x, 0, 0))]
        + [pl.BlockSpec(size, lambda x: (0, 0)) for size in sizes],
        out_shape=[jax.ShapeDtypeStruct((4, PACKET, width), jnp.bfloat16)]
        + [jax.ShapeDtypeStruct(size, jnp.bfloat16) for size in sizes],
        compiler_params=pltpu.CompilerParams(vmem_limit_bytes=62 * 2**20),
    )(place, keys, values, mask.T, queries, own_keys, own_values)
    return packet, turns[:2], turns[2:]


def put_hidden(cache_ref, hidden_ref):
    for src in range(4):
        hidden = cache_ref[src, HIDDEN, :].astype(jnp.float32)
        for b in range(4):
            hidden_ref[src, b] = jnp.broadcast_to(hidden[:, b : b + 1], (16, HEAD_DIM))


def over_cache(queries, rows, cache_ref, hidden_ref, top, total):
    product = matmul(queries, cache_ref[0, KEYS, :], NT)
    for src in range(4):
        scores = jnp.concatenate(
            [
                jnp.concatenate(
                    [
                        product[t * Q_ROWS : (t + 1) * Q_ROWS, b * BLOCK : (b + 1) * BLOCK]
                        + jnp.broadcast_to(hidden_ref[src, b, pl.ds(row, 1), :], (Q_ROWS, BLOCK))
                        for b in range(4)
                    ],
                    1,
                )
                for t, row in enumerate(rows)
            ],
            0,
        )
        if src < 3:
            product = matmul(queries, cache_ref[src + 1, KEYS, :], NT)
        top, total = fold(scores, cache_ref[src, VALUES, :], top, total)
    return top, total


def far_rows(place_ref):
    return [place_ref[t] * 4 + (1 - place_ref[5]) * 2 + place_ref[4] for t in range(4)]


def first_kernel(place_ref, f0, f1, f2, f3, mine_ref, top_ref, total_ref, hidden_ref):
    @pl.when(pl.program_id(0) == 0)
    def _():
        put_hidden(mine_ref, hidden_ref)

    queries = jnp.concatenate([tile[...] for tile in (f0, f1, f2, f3)], 0)
    top = jnp.full((4 * Q_ROWS, 1), -3e30, jnp.float32)
    total = jnp.zeros((4 * Q_ROWS, 2 * HEAD_DIM), jnp.float32)
    top, total = over_cache(queries, far_rows(place_ref), mine_ref, hidden_ref, top, total)
    top_ref[0] = jnp.broadcast_to(top, (4 * Q_ROWS, HEAD_DIM))
    total_ref[0] = total


def far_kernel(
    place_ref, f0, f1, f2, f3, theirs_ref, top_ref, total_ref, out_ref, logs_ref, hidden_ref
):
    head = pl.program_id(0)

    @pl.when(head == 0)
    def _():
        put_hidden(theirs_ref, hidden_ref)

    queries = jnp.concatenate([tile[...] for tile in (f0, f1, f2, f3)], 0)
    top = jnp.max(top_ref[0], axis=1, keepdims=True)
    top, total = over_cache(queries, far_rows(place_ref), theirs_ref, hidden_ref, top, total_ref[0])
    den = total[:, HEAD_DIM:]
    part = total[:, :HEAD_DIM] / den
    logs = top * LOG2_SCALE + jnp.log2(den)
    part = part.astype(jnp.bfloat16)
    for t in range(4):
        rows = slice(t * Q_ROWS, (t + 1) * Q_ROWS)
        out_ref[place_ref[t], pl.ds(pl.multiple_of(head * Q_ROWS, Q_ROWS), Q_ROWS), :] = part[rows]
        logs_ref[head, place_ref[t]] = logs[rows]

    @pl.when(head == HEADS_X - 1)
    def _():
        lane = lax.broadcasted_iota(jnp.int32, (Q_ROWS, HEAD_DIM), 1)
        for x in range(4):
            logs = jnp.zeros((Q_ROWS, HEAD_DIM), jnp.float32)
            for j in range(HEADS_X):
                logs = jnp.where(lane == j, logs_ref[j, x], logs)
            logs = jnp.transpose(logs)[:8]
            high = logs.astype(jnp.bfloat16).astype(jnp.float32)
            middle = (logs - high).astype(jnp.bfloat16).astype(jnp.float32)
            low = logs - high - middle
            rows = jnp.concatenate([high[:4], middle[:4], low], 0)
            rows = jnp.concatenate([rows, jnp.zeros((16, HEAD_DIM - Q_ROWS), jnp.float32)], 1)
            out_ref[x, LOGS, :] = rows.astype(jnp.bfloat16)


def near_kernel(place_ref, mine_ref, theirs_ref, top_ref, total_ref, hidden_ref):
    @pl.when(pl.program_id(0) == 0)
    def _():
        put_hidden(mine_ref, hidden_ref.at[0])
        put_hidden(theirs_ref, hidden_ref.at[1])

    mask_rows = [t * 4 + place_ref[5] * 2 + place_ref[4] for t in range(4)]
    queries = jnp.concatenate([mine_ref[x, QUERIES, :] for x in range(4)], 0)
    top = jnp.full((4 * Q_ROWS, 1), -3e30, jnp.float32)
    total = jnp.zeros((4 * Q_ROWS, 2 * HEAD_DIM), jnp.float32)
    top, total = over_cache(queries, mask_rows, mine_ref, hidden_ref.at[0], top, total)
    top, total = over_cache(queries, mask_rows, theirs_ref, hidden_ref.at[1], top, total)
    top_ref[0] = jnp.broadcast_to(top, (4 * Q_ROWS, HEAD_DIM)).reshape(4, Q_ROWS, HEAD_DIM)
    total_ref[0] = total.reshape(4, Q_ROWS, 2 * HEAD_DIM)


def own_kernel(place_ref, q_ref, o0, o1, o2, o3, top_ref, total_ref, out_ref, log_ref):
    for t, own_ref in enumerate((o0, o1, o2, o3)):
        x = place_ref[t]
        for j in range(HEADS_X):
            cols = slice(j * HEAD_DIM, (j + 1) * HEAD_DIM)
            scores = matmul(q_ref[x, :, cols], own_ref[:Q_ROWS, cols], NT)
            top = jnp.max(top_ref[j, x], axis=1, keepdims=True)
            top, total = fold(scores, own_ref[Q_ROWS:, cols], top, total_ref[j, x])
            den = total[:, HEAD_DIM:]
            out_ref[j, x] = total[:, :HEAD_DIM] / den
            log_ref[j, x] = top * LOG2_SCALE + jnp.log2(den)


def join_kernel(near_ref, near_log_ref, far_ref, out_ref):
    for x in range(4):
        logs = far_ref[x, LOGS, :].astype(jnp.float32)
        logs = logs[:4] + logs[4:8] + logs[8:12]
        logs = jnp.transpose(jnp.concatenate([logs, logs], 0))
        for j in range(HEADS_X):
            far_log = logs[:Q_ROWS, j : j + 1]
            near_log = near_log_ref[j, x]
            top = jnp.maximum(near_log, far_log)
            near_share, far_share = jnp.exp2(near_log - top), jnp.exp2(far_log - top)
            far = far_ref[x, j * Q_ROWS : (j + 1) * Q_ROWS, :].astype(jnp.float32)
            value = (near_ref[j, x] * near_share + far * far_share) / (near_share + far_share)
            value = value.astype(jnp.bfloat16)
            for y in range(4):
                out_ref[x * 4 + y, j * 16 : (j + 1) * 16, :] = value[y * 16 : (y + 1) * 16]


def norm_kernel(part_ref, gain_ref, out_ref):
    squares = jnp.zeros((16, HEAD_DIM), jnp.float32)
    for src in range(16):
        value = part_ref[src].astype(jnp.float32)
        value = value * value
        for j in range(HEADS_X):
            squares = squares + value[j * 16 : (j + 1) * 16]
    mean = jnp.sum(squares, axis=1, keepdims=True) * (1.0 / 6144)
    factor = lax.rsqrt(mean + 1e-06)
    for x in range(4):
        for y in range(4):
            for j in range(HEADS_X):
                value = part_ref[x * 4 + y, j * 16 : (j + 1) * 16, :].astype(jnp.float32)
                place = (y * 12 + x * HEADS_X + j) * HEAD_DIM
                cols = slice(place, place + HEAD_DIM)
                gain = gain_ref[:, cols].astype(jnp.float32)
                out_ref[:, cols] = (value * factor * gain).astype(jnp.bfloat16)


def attend(place, far, own, mine, theirs):
    heads = HEADS_X
    tiles = [pl.BlockSpec((Q_ROWS, HEAD_DIM), lambda j, row=row: (row, j)) for row in (0, 0, 0, 1)]
    cache = pl.BlockSpec((4, PACKET, HEAD_DIM), lambda j: (0, 0, j))

    state = [
        pl.BlockSpec((1, 4 * Q_ROWS, width), lambda j: (j, 0, 0)) for width in (HEAD_DIM, 2 * HEAD_DIM)
    ]
    state_shape = [
        jax.ShapeDtypeStruct((heads, 4 * Q_ROWS, width), jnp.float32) for width in (HEAD_DIM, 2 * HEAD_DIM)
    ]
    hidden = pltpu.VMEM((4, 4, 16, HEAD_DIM), jnp.float32)

    def common(keys):
        return dict(
            grid=(heads,),
            compiler_params=PARAMS,
            cost_estimate=pl.CostEstimate(
                flops=heads * 16 * Q_ROWS * keys * 128,
                bytes_accessed=heads * keys * 2**9,
                transcendentals=heads * 4 * Q_ROWS * keys,
            ),
        )

    top, total = pl.pallas_call(
        first_kernel,
        in_specs=[SMEM] + tiles + [cache],
        out_specs=state,
        out_shape=state_shape,
        scratch_shapes=[hidden],
        **common(2048),
    )(place, *far, mine)
    far_out = pl.pallas_call(
        far_kernel,
        in_specs=[SMEM] + tiles + [cache] + state,
        out_specs=pl.BlockSpec((4, FAR, HEAD_DIM), lambda j: (0, 0, 0)),
        out_shape=jax.ShapeDtypeStruct((4, FAR, HEAD_DIM), jnp.bfloat16),
        scratch_shapes=[pltpu.VMEM((heads, 4, Q_ROWS, HEAD_DIM), jnp.float32), hidden],
        **common(2048),
    )(place, *far, theirs, top, total)
    far_out, own[1], own[2] = lax.optimization_barrier((far_out, own[1], own[2]))
    far_out = lax.ppermute(far_out, "z", [(0, 1), (1, 0)])
    for turn in (1, 2):
        own[turn] = lax.ppermute(own[turn], "x", [(x, (x + turn) % 4) for x in range(4)])
    near = [
        pl.BlockSpec((1, 4, Q_ROWS, width), lambda j: (j, 0, 0, 0)) for width in (HEAD_DIM, 2 * HEAD_DIM)
    ]
    top, total = pl.pallas_call(
        near_kernel,
        in_specs=[SMEM, cache, cache],
        out_specs=near,
        out_shape=[
            jax.ShapeDtypeStruct((heads, 4, Q_ROWS, width), jnp.float32) for width in (HEAD_DIM, 2 * HEAD_DIM)
        ],
        scratch_shapes=[pltpu.VMEM((2, 4, 4, 16, HEAD_DIM), jnp.float32)],
        **common(4096),
    )(place, mine, theirs)

    def whole(shape):
        return pl.BlockSpec(shape, lambda i: (0,) * len(shape))

    near_shape = (heads, 4, Q_ROWS, HEAD_DIM)
    near_out, near_log = pl.pallas_call(
        own_kernel,
        grid=(1,),
        in_specs=[
            SMEM,
            pl.BlockSpec((4, Q_ROWS, heads * HEAD_DIM), lambda i: (0, QUERIES.start // Q_ROWS, 0)),
            *[whole((2 * Q_ROWS, heads * HEAD_DIM))] * 4,
            whole(top.shape),
            whole(total.shape),
        ],
        out_specs=[whole(near_shape)] * 2,
        out_shape=[jax.ShapeDtypeStruct(near_shape, jnp.float32)] * 2,
        compiler_params=PARAMS,
    )(place, mine, *own, top, total)
    return pl.pallas_call(
        join_kernel,
        in_specs=[VMEM] * 3,
        out_specs=VMEM,
        out_shape=jax.ShapeDtypeStruct((16, heads * 16, HEAD_DIM), jnp.bfloat16),
        compiler_params=PARAMS,
    )(near_out, near_log, far_out)


def local(queries, group_keys, group_values, cache_keys, cache_values, block_mask, gain):
    me, z, core = (lax.axis_index(axis) for axis in ("x", "z", "core"))
    place = [(me - turn) % 4 for turn in range(4)] + [core, z] + [(me + turn) % 4 for turn in range(4)]
    place = jnp.stack(place).astype(jnp.int32)

    packet, blocks, own = pack(
        place, cache_keys, cache_values, block_mask, queries, group_keys, group_values
    )
    mine = lax.all_to_all(packet, "x", 0, 0, tiled=True)

    def send(block, turn):
        route = [(x * 2 + z, (x + turn) % 4 * 2 + 1 - z) for x in range(4) for z in range(2)]
        return lax.ppermute(block, ("x", "z"), route)

    far = [send(blocks[0], 0), send(blocks[1], 2)]
    odd = jnp.concatenate([block[Q_ROWS:] for block in far], 0)
    odd = lax.ppermute(odd, "x", [(x, (x + 1) % 4) for x in range(4)])
    own[3] = lax.ppermute(own[3], "x", [(x, (x + 3) % 4) for x in range(4)])
    mine, far, own[3] = lax.optimization_barrier((mine, [far[0], odd, far[1]], own[3]))
    far = [pltpu.with_memory_space_constraint(a, pltpu.HBM) for a in far]
    far.append(far[1])
    theirs = lax.ppermute(mine, "core", [(0, 1), (1, 0)])
    block = attend(place, far, own, mine, theirs)
    block = lax.all_to_all(block, ("x", "head"), 0, 0, tiled=True)
    return pl.pallas_call(
        norm_kernel,
        in_specs=[VMEM] * 2,
        out_specs=VMEM,
        out_shape=jax.ShapeDtypeStruct((16, 48 * HEAD_DIM), jnp.bfloat16),
        compiler_params=PARAMS,
    )(block, gain.reshape(1, 48 * HEAD_DIM))


def solution(mesh):
    fine = Mesh(mesh.devices.reshape(8, 4, 2, 2, 4), ("video", "x", "z", "core", "head"))
    rows = ("video", "x", "z", "core")
    return jax.shard_map(
        local,
        mesh=fine,
        in_specs=(P(rows, "head"),) * 5 + (P("video", ("x", "z", "core")), P()),
        out_specs=P((*rows, "head"), None),
        check_vma=False,
    )
```
